32 devices in a mesh: kpt: 2 (over y), pert: 4 (over z), pw: 4 (over x, core).
Axes of the slice: x: 2, y: 2, z: 4, core: 2. Of those that a mesh axis runs over, the one named last changes fastest.
Arguments:
- occupied: bfloat16 [3072, 8192], P(('kpt', 'pert'), 'pw'), parts along dimension 0, may hold values from -0.0625 to 0.0625
- response: bfloat16 [8, 128, 8192], P(('kpt', 'pert'), None, 'pw'), parts along dimension 0, may hold values from -6 to 6
Outputs:
- correlation: float32 [8, 128, 1536], P(('kpt', 'pert')), parts along dimension 0
- projected: float32 [8, 128, 8192], P(('kpt', 'pert'), None, 'pw'), parts along dimension 0
The draws below stay inside these ranges and needn't reach their ends.
There are 2 independent parts, one for each index of `kpt`. The reference program is written for one: setup_inputs(seed, part) draws one part's arguments, and reference() takes and returns one part's arrays. A program takes and returns all parts, laid end to end along the dimension named above; each array names one. Nothing has to cross between parts.
All inputs are finite; a program needn't handle non-finite values.
Results may differ from the reference program's by a relative error of at most 0.00096.
Values may be sent and summed in bfloat16 or wider, within the bound.
A program may use at most 64 MiB of HBM per device.

```python
import jax
import jax.numpy as jnp
from jax import lax

NB = 1536
RB = 128
NPW = 8192
NPERT = 4


def steps_of(own_key, shape, split, low, largest):
    def one(axis_at, shards_of):
        steps = jax.random.uniform(jax.random.fold_in(jax.random.fold_in(own_key, 6), axis_at), (shards_of,), jnp.float32, low / len(split), largest / len(split))
        return jnp.repeat(jnp.exp(steps), shape[axis_at] // shards_of).reshape((-1,) + (1,) * (len(shape) - axis_at - 1))

    gain = one(*split[0])
    for cut in split[1:]:
        gain = gain * one(*cut)
    return gain


def centred(stream_key, extent, spread, bound, pieces=(), dtype=jnp.bfloat16):
    drawn = spread * jax.random.normal(stream_key, extent, jnp.float32)
    if pieces:
        drawn = drawn * steps_of(stream_key, extent, pieces, -0.22, 0.18)
    return jnp.clip(drawn, -bound, bound).astype(dtype)


def setup_inputs(seed: int = 0, part: int = 0) -> dict:
    seeds = jax.random.split(jax.random.key(seed), 3)
    own_keys = jax.random.split(jax.random.fold_in(seeds[2], part), 3)
    occupied = centred(own_keys[0], (NB, NPW), NPW ** -0.5, 0.0625, ((0, 4), (1, 4)))
    response = centred(own_keys[1], (NPERT, RB, NPW), 1.0, 6.0, ((0, 4), (2, 4)))
    return {"occupied": occupied, "response": response}


def reference(occupied, response):
    def one_perturbation(resp):
        correlation = lax.dot_general(resp, occupied, (((1,), (1,)), ((), ())), preferred_element_type=jnp.float32)
        weights = correlation.astype(jnp.bfloat16)
        correction = jnp.dot(weights, occupied, preferred_element_type=jnp.float32)
        return correlation, resp.astype(jnp.float32) - correction

    correlation, projected = lax.map(one_perturbation, response)
    return correlation, projected
```

```python
import functools

import jax
import jax.numpy as jnp
from jax import lax
from jax.experimental import pallas as pl
from jax.experimental.pallas import tpu as pltpu
from jax.sharding import PartitionSpec as P

CHUNKS = 4
MESH = pl.DeviceIdType.MESH
NT = (((1,), (1,)), ((), ()))


def kernel(n, width, occ, resp, cout, proj, r_all, cp, rs, wgt, cs, chome, down, narrow, got, last,
           r_send, r_recv, rs_send, rs_recv, ag_send, ag_recv, h_send, h_recv, o_send, o_recv,
           d_send, d_recv, l_recv):
    bands = occ.shape[0]
    rows, cols = resp.shape
    tile = cols // CHUNKS
    me = lax.axis_index("pert")
    mine = lax.axis_index("pw")

    barrier = pltpu.get_barrier_semaphore()
    for k in range(1, n):
        pl.semaphore_signal(barrier, inc=1, device_id={"pert": lax.rem(me + k, n)}, device_id_type=MESH)
    for k in range(1, width):
        pl.semaphore_signal(barrier, inc=1, device_id={"pw": lax.rem(mine + k, width)}, device_id_type=MESH)
    pl.semaphore_wait(barrier, n + width - 2)

    def response_copy(src, q, side):
        return pltpu.make_async_remote_copy(
            src_ref=src, dst_ref=r_all.at[q], send_sem=r_send.at[side, q], recv_sem=r_recv.at[q],
            device_id={"pert": me + 2 * side - 1}, device_id_type=MESH)

    def partial_copy(q, peer):
        return pltpu.make_async_remote_copy(
            src_ref=cp.at[q, peer], dst_ref=rs.at[q, mine], send_sem=rs_send.at[q, peer],
            recv_sem=rs_recv.at[q, mine], device_id={"pw": peer}, device_id_type=MESH)

    def weight_copy(q, peer):
        return pltpu.make_async_remote_copy(
            src_ref=wgt.at[q, mine], dst_ref=wgt.at[q, mine], send_sem=ag_send.at[q, peer],
            recv_sem=ag_recv.at[q, mine], device_id={"pw": peer}, device_id_type=MESH)

    def home_copy(q):
        return pltpu.make_async_remote_copy(
            src_ref=cs.at[q], dst_ref=chome.at[me], send_sem=h_send.at[q], recv_sem=h_recv.at[me],
            device_id={"pert": q}, device_id_type=MESH)

    def spread_copy(j, peer):
        where = cout.at[mine, :, pl.ds(pl.multiple_of(j * bands, 128), bands)]
        return pltpu.make_async_remote_copy(
            src_ref=chome.at[j], dst_ref=where, send_sem=o_send.at[j, peer],
            recv_sem=o_recv.at[j, mine], device_id={"pw": peer}, device_id_type=MESH)

    def narrow_copy(q, c):
        return pltpu.make_async_remote_copy(
            src_ref=narrow.at[q, c], dst_ref=got.at[q, c], send_sem=d_send.at[q, c],
            recv_sem=d_recv.at[q, c], device_id={"pert": jnp.where(q < me, me - 1, me + 1)},
            device_id_type=MESH)

    def last_copy(q, c):
        side = jnp.where(q < me, 0, 1)
        return pltpu.make_async_remote_copy(
            src_ref=down.at[q, c], dst_ref=last.at[side, c], send_sem=d_send.at[q, c],
            recv_sem=l_recv.at[side, c], device_id={"pert": q}, device_id_type=MESH)

    def arrived(ref, sem):
        pltpu.make_async_copy(ref, ref, sem).wait()

    def is_next(q):
        return (q == me - 1) | (q == me + 1)

    def send_correction(q, c, value):
        @pl.when(is_next(q))
        def _():
            down[q, c] = value
            last_copy(q, c).start()

        @pl.when(jnp.logical_not(is_next(q)))
        def _():
            narrow[q, c] = value.astype(narrow.dtype)
            narrow_copy(q, c).start()

    for side in range(2):
        @pl.when((me > 0) if side == 0 else (me < n - 1))
        def _(side=side):
            response_copy(resp, me, side).start()
    r_all[me] = resp[...]

    def process(q):
        part = lax.dot_general(r_all[q], occ[...], NT, preferred_element_type=jnp.float32)
        cp[q] = part.reshape(cp.shape[1:])
        for k in range(1, width):
            partial_copy(q, lax.rem(mine + k, width)).start()
        rs[q, mine] = cp[q, mine]
        for k in range(1, width):
            src = lax.rem(mine + k, width)
            arrived(rs.at[q, src], rs_recv.at[q, src])
        total = rs[q, 0]
        for k in range(1, width):
            total = total + rs[q, k]
        wgt[q, mine] = total.astype(wgt.dtype)
        for k in range(1, width):
            weight_copy(q, lax.rem(mine + k, width)).start()

        @pl.when(q == me)
        def _():
            chome[q] = total

        @pl.when(q != me)
        def _():
            cs[q] = total
            home_copy(q).start()

        for k in range(1, width):
            src = lax.rem(mine + k, width)
            arrived(wgt.at[q, src], ag_recv.at[q, src])
        weights = wgt[q].reshape(rows, bands)
        source = ((q < me) & (me == n - 1)) | ((q > me) & (me == 0))
        for c in range(CHUNKS):
            value = jnp.dot(weights, occ[:, c * tile:(c + 1) * tile], preferred_element_type=jnp.float32)

            @pl.when(source)
            def _(c=c, value=value):
                send_correction(q, c, value)

            @pl.when(jnp.logical_not(source))
            def _(c=c, value=value):
                down[q, c] = value

    def relay(step):
        for c in range(CHUNKS):
            for side in range(2):
                q = n - 1 - step if side == 0 else step
                between = ((q < me) & (me < n - 1)) if side == 0 else ((q > me) & (me > 0))

                @pl.when(between)
                def _(c=c, q=q):
                    arrived(got.at[q, c], d_recv.at[q, c])
                    send_correction(q, c, down[q, c] + got[q, c].astype(jnp.float32))

    def spread(step):
        def one(side, _):
            j = me + step * (2 * side - 1)

            @pl.when((j >= 0) & (j < n) & ((side == 0) | (step > 0)))
            def _():
                @pl.when(j != me)
                def _():
                    arrived(chome.at[j], h_recv.at[j])

                for k in range(1, width):
                    spread_copy(j, lax.rem(mine + k, width)).start()
                cout[mine, :, pl.ds(pl.multiple_of(j * bands, 128), bands)] = chome[j]
            return 0

        lax.fori_loop(0, 2, one, 0)

    def turn(step, _):
        def one(side, _):
            q = me + step * (2 * side - 1)

            @pl.when((q >= 0) & (q < n) & ((side == 0) | (step > 0)))
            def _():
                @pl.when(q != me)
                def _():
                    arrived(r_all.at[q], r_recv.at[q])

                    @pl.when((side == 0) & (me < n - 1))
                    def _():
                        response_copy(r_all.at[q], q, 1).start()

                    @pl.when((side == 1) & (me > 0))
                    def _():
                        response_copy(r_all.at[q], q, 0).start()

                process(q)
            return 0

        lax.fori_loop(0, 2, one, 0)

        @pl.when(step > 0)
        def _():
            relay(step - 1)
            spread(step - 1)
        return 0

    lax.fori_loop(0, n, turn, 0)
    relay(n - 1)
    spread(n - 1)

    for c in range(CHUNKS):
        at = slice(c * tile, (c + 1) * tile)
        proj[:, at] = down[me, c]

        for side in range(2):
            @pl.when((me < n - 1) if side == 0 else (me > 0))
            def _(side=side, at=at, c=c):
                arrived(last.at[side, c], l_recv.at[side, c])
                proj[:, at] = proj[:, at] + last[side, c]

        proj[:, at] = resp[:, at].astype(jnp.float32) - proj[:, at]

    def drain(q, _):
        for k in range(1, width):
            peer = lax.rem(mine + k, width)
            partial_copy(q, peer).wait_send()
            weight_copy(q, peer).wait_send()
            spread_copy(q, peer).wait_send()
            arrived(cout.at[peer, :, pl.ds(pl.multiple_of(q * bands, 128), bands)], o_recv.at[q, peer])

        @pl.when((q >= me) & (me > 0))
        def _():
            response_copy(r_all.at[q], q, 0).wait_send()

        @pl.when((q <= me) & (me < n - 1))
        def _():
            response_copy(r_all.at[q], q, 1).wait_send()

        @pl.when(q != me)
        def _():
            home_copy(q).wait_send()
            for c in range(CHUNKS):
                @pl.when(is_next(q))
                def _(c=c):
                    last_copy(q, c).wait_send()

                @pl.when(jnp.logical_not(is_next(q)))
                def _(c=c):
                    narrow_copy(q, c).wait_send()
        return 0

    lax.fori_loop(0, n, drain, 0)


def fused(occupied, rows):
    n, width = lax.axis_size("pert"), lax.axis_size("pw")
    count, cols = rows.shape
    bands = occupied.shape[0]
    part, tile = count // width, cols // CHUNKS
    f32, bf16 = jnp.float32, jnp.bfloat16
    dma = pltpu.SemaphoreType.DMA
    vmem = pl.BlockSpec(memory_space=pltpu.VMEM)
    correlation, projected = pl.pallas_call(
        functools.partial(kernel, n, width),
        out_shape=(
            jax.ShapeDtypeStruct((width, part, n * bands), f32),
            jax.ShapeDtypeStruct((count, cols), f32),
        ),
        in_specs=[vmem] * 2,
        out_specs=(vmem, vmem),
        scratch_shapes=[
            pltpu.VMEM((n, count, cols), bf16),
            pltpu.VMEM((n, width, part, bands), f32),
            pltpu.VMEM((n, width, part, bands), f32),
            pltpu.VMEM((n, width, part, bands), bf16),
            pltpu.VMEM((n, part, bands), f32),
            pltpu.VMEM((n, part, bands), f32),
            pltpu.VMEM((n, CHUNKS, count, tile), f32),
            pltpu.VMEM((n, CHUNKS, count, tile), bf16),
            pltpu.VMEM((n, CHUNKS, count, tile), bf16),
            pltpu.VMEM((2, CHUNKS, count, tile), f32),
            dma((2, n)), dma((n,)),
            dma((n, width)), dma((n, width)),
            dma((n, width)), dma((n, width)),
            dma((n,)), dma((n,)),
            dma((n, width)), dma((n, width)),
            dma((n, CHUNKS)), dma((n, CHUNKS)), dma((2, CHUNKS)),
        ],
        compiler_params=pltpu.CompilerParams(
            collective_id=0, has_side_effects=True, vmem_limit_bytes=48 * 2**20
        ),
    )(occupied, rows)
    return correlation.reshape(count, n * bands), projected


def ring(occupied, rows):
    band_local = occupied.shape[0]
    n = lax.axis_size("pert")
    position = lax.axis_index("pert")
    zero = jnp.zeros((), jnp.int32)

    def visit(step, piece, correlation, correction):
        start = (position - step) % n * band_local
        part = lax.dot_general(rows, piece, NT, preferred_element_type=jnp.float32)
        summed = lax.psum(part, "pw")
        correlation = lax.dynamic_update_slice(correlation, summed, (zero, start))
        correction = correction + jnp.dot(
            summed.astype(jnp.bfloat16), piece, preferred_element_type=jnp.float32
        )
        return correlation, correction

    def turn(step, state):
        piece, correlation, correction = state
        correlation, correction = visit(step, piece, correlation, correction)
        piece = lax.ppermute(piece, "pert", [(i, (i + 1) % n) for i in range(n)])
        return piece, correlation, correction

    state = (occupied, jnp.zeros((rows.shape[0], n * band_local), jnp.float32), jnp.zeros(rows.shape, jnp.float32))
    piece, correlation, correction = lax.fori_loop(0, n - 1, turn, state)
    correlation, correction = visit(n - 1, piece, correlation, correction)
    return correlation, rows.astype(jnp.float32) - correction


def local(occupied, response):
    rows = response.reshape(-1, response.shape[-1])
    small = rows.shape[0] <= occupied.shape[0]
    even = occupied.shape[0] % 128 == 0 and rows.shape[0] % (16 * lax.axis_size("pw")) == 0
    body = fused if small and even and rows.shape[1] % (128 * CHUNKS) == 0 else ring
    correlation, projected = body(occupied, rows)
    return correlation.reshape(response.shape[:2] + correlation.shape[1:]), projected.reshape(response.shape)


def solution(mesh):
    in_specs = (P(("kpt", "pert"), "pw"), P(("kpt", "pert"), None, "pw"))
    out_specs = (P(("kpt", "pert"), None, None), P(("kpt", "pert"), None, "pw"))
    return jax.shard_map(local, mesh=mesh, in_specs=in_specs, out_specs=out_specs, check_vma=False)
```

```python
import functools

import jax
import jax.numpy as jnp
from jax import lax
from jax.experimental import pallas as pl
from jax.experimental.pallas import tpu as pltpu
from jax.sharding import PartitionSpec as P

CHUNKS = 4
MESH = pl.DeviceIdType.MESH
NT = (((1,), (1,)), ((), ()))


def kernel(n, width, occ_far, resp_far, cout, proj, occ, r_all, cp, rs, wgt, cs, chome, down, narrow, got,
           last, in_sem, r_send, r_recv, rs_send, rs_recv, ag_send, ag_recv, h_send, h_recv, o_send, o_recv,
           d_send, d_recv, f_send, l_recv):
    bands = occ.shape[0]
    rows, cols = resp_far.shape
    tile = cols // CHUNKS
    me = lax.axis_index("pert")
    mine = lax.axis_index("pw")

    bring_rows = pltpu.make_async_copy(resp_far, r_all.at[me], in_sem.at[0])
    bring_bands = pltpu.make_async_copy(occ_far, occ, in_sem.at[1])
    bring_rows.start()
    bring_bands.start()
    barrier = pltpu.get_barrier_semaphore()
    for k in range(1, n):
        pl.semaphore_signal(barrier, inc=1, device_id={"pert": lax.rem(me + k, n)}, device_id_type=MESH)
    for k in range(1, width):
        pl.semaphore_signal(barrier, inc=1, device_id={"pw": lax.rem(mine + k, width)}, device_id_type=MESH)
    bring_rows.wait()
    pl.semaphore_wait(barrier, n + width - 2)

    def response_copy(q, side):
        return pltpu.make_async_remote_copy(
            src_ref=r_all.at[q], dst_ref=r_all.at[q], send_sem=r_send.at[side, q], recv_sem=r_recv.at[q],
            device_id={"pert": me + 2 * side - 1}, device_id_type=MESH)

    def partial_copy(q, peer):
        return pltpu.make_async_remote_copy(
            src_ref=cp.at[q, peer], dst_ref=rs.at[q, mine], send_sem=rs_send.at[q, peer],
            recv_sem=rs_recv.at[q, mine], device_id={"pw": peer}, device_id_type=MESH)

    def weight_copy(q, peer):
        return pltpu.make_async_remote_copy(
            src_ref=wgt.at[q, mine], dst_ref=wgt.at[q, mine], send_sem=ag_send.at[q, peer],
            recv_sem=ag_recv.at[q, mine], device_id={"pw": peer}, device_id_type=MESH)

    def home_copy(q):
        return pltpu.make_async_remote_copy(
            src_ref=cs.at[q], dst_ref=chome.at[me], send_sem=h_send.at[q], recv_sem=h_recv.at[me],
            device_id={"pert": q}, device_id_type=MESH)

    def spread_copy(j, peer):
        where = cout.at[mine, :, pl.ds(pl.multiple_of(j * bands, 128), bands)]
        return pltpu.make_async_remote_copy(
            src_ref=chome.at[j], dst_ref=where, send_sem=o_send.at[j, peer],
            recv_sem=o_recv.at[j, mine], device_id={"pw": peer}, device_id_type=MESH)

    def narrow_copy(q, c):
        return pltpu.make_async_remote_copy(
            src_ref=narrow.at[q, c], dst_ref=got.at[q, c], send_sem=d_send.at[q, c],
            recv_sem=d_recv.at[q, c], device_id={"pert": jnp.where(q < me, me - 1, me + 1)},
            device_id_type=MESH)

    def last_copy(q, c):
        side = jnp.where(q < me, 0, 1)
        return pltpu.make_async_remote_copy(
            src_ref=narrow.at[q, c], dst_ref=last.at[side, 0, c], send_sem=d_send.at[q, c],
            recv_sem=l_recv.at[side, 0, c], device_id={"pert": q}, device_id_type=MESH)

    def forward_copy(q, c):
        side = jnp.where(q < me, 0, 1)
        return pltpu.make_async_remote_copy(
            src_ref=got.at[q, c], dst_ref=last.at[side, 1, c], send_sem=f_send.at[q, c],
            recv_sem=l_recv.at[side, 1, c], device_id={"pert": q}, device_id_type=MESH)

    def arrived(ref, sem):
        pltpu.make_async_copy(ref, ref, sem).wait()

    def is_next(q):
        return (q == me - 1) | (q == me + 1)

    for side in range(2):
        @pl.when((me > 0) if side == 0 else (me < n - 1))
        def _(side=side):
            response_copy(me, side).start()
    bring_bands.wait()

    def process(q):
        part = lax.dot_general(r_all[q], occ[...], NT, preferred_element_type=jnp.float32)
        cp[q] = part.reshape(cp.shape[1:])
        for k in range(1, width):
            partial_copy(q, lax.rem(mine + k, width)).start()
        rs[q, mine] = cp[q, mine]
        for k in range(1, width):
            src = lax.rem(mine + k, width)
            arrived(rs.at[q, src], rs_recv.at[q, src])
        total = rs[q, 0]
        for k in range(1, width):
            total = total + rs[q, k]
        wgt[q, mine] = total.astype(wgt.dtype)
        for k in range(1, width):
            weight_copy(q, lax.rem(mine + k, width)).start()

        @pl.when(q == me)
        def _():
            chome[q] = total

        @pl.when(q != me)
        def _():
            cs[q] = total
            home_copy(q).start()

        for k in range(1, width):
            src = lax.rem(mine + k, width)
            arrived(wgt.at[q, src], ag_recv.at[q, src])
        weights = wgt[q].reshape(rows, bands)
        source = ((q < me) & (me == n - 1)) | ((q > me) & (me == 0))
        for c in range(CHUNKS):
            value = jnp.dot(weights, occ[:, c * tile:(c + 1) * tile], preferred_element_type=jnp.float32)

            @pl.when(source | is_next(q))
            def _(c=c, value=value):
                narrow[q, c] = value.astype(narrow.dtype)

            @pl.when(source & is_next(q))
            def _(c=c):
                last_copy(q, c).start()

            @pl.when(source & jnp.logical_not(is_next(q)))
            def _(c=c):
                narrow_copy(q, c).start()

            @pl.when(jnp.logical_not(source | is_next(q)))
            def _(c=c, value=value):
                down[q, c] = value

    def launch(step):
        for side in range(2):
            inner = (me > 0) & (me < n - 1)
            final = n - me if side == 0 else me + 1

            @pl.when(inner & (step == final))
            def _(side=side):
                response_copy(n - 1 if side == 0 else 0, side).wait_send()
                for c in range(CHUNKS):
                    last_copy(me + 2 * side - 1, c).start()

    def relay(step):
        for c in range(CHUNKS):
            for side in range(2):
                q = n - 1 - step if side == 0 else step
                between = ((q < me) & (me < n - 1)) if side == 0 else ((q > me) & (me > 0))

                @pl.when(between)
                def _(c=c, q=q):
                    arrived(got.at[q, c], d_recv.at[q, c])

                    @pl.when(is_next(q))
                    def _():
                        forward_copy(q, c).start()

                    @pl.when(jnp.logical_not(is_next(q)))
                    def _():
                        total = down[q, c] + got[q, c].astype(jnp.float32)
                        narrow[q, c] = total.astype(narrow.dtype)
                        narrow_copy(q, c).start()

    def spread(step):
        def one(side, _):
            j = me + step * (2 * side - 1)

            @pl.when((j >= 0) & (j < n) & ((side == 0) | (step > 0)))
            def _():
                @pl.when(j != me)
                def _():
                    arrived(chome.at[j], h_recv.at[j])

                for k in range(1, width):
                    spread_copy(j, lax.rem(mine + k, width)).start()
                cout[mine, :, pl.ds(pl.multiple_of(j * bands, 128), bands)] = chome[j]
            return 0

        lax.fori_loop(0, 2, one, 0)

    def turn(step, _):
        launch(step)

        def one(side, _):
            q = me + step * (2 * side - 1)

            @pl.when((q >= 0) & (q < n) & ((side == 0) | (step > 0)))
            def _():
                @pl.when(q != me)
                def _():
                    arrived(r_all.at[q], r_recv.at[q])

                    @pl.when((side == 0) & (me < n - 1))
                    def _():
                        response_copy(q, 1).start()

                    @pl.when((side == 1) & (me > 0))
                    def _():
                        response_copy(q, 0).start()

                process(q)
            return 0

        lax.fori_loop(0, 2, one, 0)

        @pl.when(step > 0)
        def _():
            relay(step - 1)
            spread(step - 1)
        return 0

    lax.fori_loop(0, n, turn, 0)
    launch(n)
    relay(n - 1)
    spread(n - 1)

    for c in range(CHUNKS):
        at = slice(c * tile, (c + 1) * tile)
        proj[:, at] = down[me, c]

        for side in range(2):
            for k in range(2):
                @pl.when((me < n - 1 - k) if side == 0 else (me > k))
                def _(side=side, k=k, at=at, c=c):
                    arrived(last.at[side, k, c], l_recv.at[side, k, c])
                    proj[:, at] = proj[:, at] + last[side, k, c].astype(jnp.float32)

        proj[:, at] = r_all[me, :, at].astype(jnp.float32) - proj[:, at]

    def drain(q, _):
        for k in range(1, width):
            peer = lax.rem(mine + k, width)
            partial_copy(q, peer).wait_send()
            weight_copy(q, peer).wait_send()
            spread_copy(q, peer).wait_send()
            arrived(cout.at[peer, :, pl.ds(pl.multiple_of(q * bands, 128), bands)], o_recv.at[q, peer])

        inner = (me > 0) & (me < n - 1)

        @pl.when((q >= me) & (me > 0) & jnp.logical_not(inner & (q == n - 1)))
        def _():
            response_copy(q, 0).wait_send()

        @pl.when((q <= me) & (me < n - 1) & jnp.logical_not(inner & (q == 0)))
        def _():
            response_copy(q, 1).wait_send()

        @pl.when(q != me)
        def _():
            home_copy(q).wait_send()
            for c in range(CHUNKS):
                @pl.when(is_next(q))
                def _(c=c):
                    last_copy(q, c).wait_send()

                    @pl.when(inner)
                    def _():
                        forward_copy(q, c).wait_send()

                @pl.when(jnp.logical_not(is_next(q)))
                def _(c=c):
                    narrow_copy(q, c).wait_send()
        return 0

    lax.fori_loop(0, n, drain, 0)


def fused(occupied, rows):
    n, width = lax.axis_size("pert"), lax.axis_size("pw")
    count, cols = rows.shape
    bands = occupied.shape[0]
    part, tile = count // width, cols // CHUNKS
    f32, bf16 = jnp.float32, jnp.bfloat16
    dma = pltpu.SemaphoreType.DMA
    vmem = pl.BlockSpec(memory_space=pltpu.VMEM)
    correlation, projected = pl.pallas_call(
        functools.partial(kernel, n, width),
        out_shape=(
            jax.ShapeDtypeStruct((width, part, n * bands), f32),
            jax.ShapeDtypeStruct((count, cols), f32),
        ),
        in_specs=[pl.BlockSpec(memory_space=pltpu.HBM)] * 2,
        out_specs=(vmem, vmem),
        scratch_shapes=[
            pltpu.VMEM((bands, cols), bf16),
            pltpu.VMEM((n, count, cols), bf16),
            pltpu.VMEM((n, width, part, bands), f32),
            pltpu.VMEM((n, width, part, bands), f32),
            pltpu.VMEM((n, width, part, bands), bf16),
            pltpu.VMEM((n, part, bands), f32),
            pltpu.VMEM((n, part, bands), f32),
            pltpu.VMEM((n, CHUNKS, count, tile), f32),
            pltpu.VMEM((n, CHUNKS, count, tile), bf16),
            pltpu.VMEM((n, CHUNKS, count, tile), bf16),
            pltpu.VMEM((2, 2, CHUNKS, count, tile), bf16),
            dma((2,)), dma((2, n)), dma((n,)),
            dma((n, width)), dma((n, width)),
            dma((n, width)), dma((n, width)),
            dma((n,)), dma((n,)),
            dma((n, width)), dma((n, width)),
            dma((n, CHUNKS)), dma((n, CHUNKS)), dma((n, CHUNKS)), dma((2, 2, CHUNKS)),
        ],
        compiler_params=pltpu.CompilerParams(
            collective_id=0, has_side_effects=True, vmem_limit_bytes=48 * 2**20
        ),
    )(occupied, rows)
    return correlation.reshape(count, n * bands), projected


def ring(occupied, rows):
    band_local = occupied.shape[0]
    n = lax.axis_size("pert")
    position = lax.axis_index("pert")
    zero = jnp.zeros((), jnp.int32)

    def visit(step, piece, correlation, correction):
        start = (position - step) % n * band_local
        part = lax.dot_general(rows, piece, NT, preferred_element_type=jnp.float32)
        summed = lax.psum(part, "pw")
        correlation = lax.dynamic_update_slice(correlation, summed, (zero, start))
        correction = correction + jnp.dot(
            summed.astype(jnp.bfloat16), piece, preferred_element_type=jnp.float32
        )
        return correlation, correction

    def turn(step, state):
        piece, correlation, correction = state
        correlation, correction = visit(step, piece, correlation, correction)
        piece = lax.ppermute(piece, "pert", [(i, (i + 1) % n) for i in range(n)])
        return piece, correlation, correction

    state = (occupied, jnp.zeros((rows.shape[0], n * band_local), jnp.float32), jnp.zeros(rows.shape, jnp.float32))
    piece, correlation, correction = lax.fori_loop(0, n - 1, turn, state)
    correlation, correction = visit(n - 1, piece, correlation, correction)
    return correlation, rows.astype(jnp.float32) - correction


def local(occupied, response):
    rows = response.reshape(-1, response.shape[-1])
    small = rows.shape[0] <= occupied.shape[0]
    even = occupied.shape[0] % 128 == 0 and rows.shape[0] % (16 * lax.axis_size("pw")) == 0
    body = fused if small and even and rows.shape[1] % (128 * CHUNKS) == 0 else ring
    correlation, projected = body(occupied, rows)
    return correlation.reshape(response.shape[:2] + correlation.shape[1:]), projected.reshape(response.shape)


def solution(mesh):
    in_specs = (P(("kpt", "pert"), "pw"), P(("kpt", "pert"), None, "pw"))
    out_specs = (P(("kpt", "pert"), None, None), P(("kpt", "pert"), None, "pw"))
    return jax.shard_map(local, mesh=mesh, in_specs=in_specs, out_specs=out_specs, check_vma=False)
```

```python
import functools

import jax
import jax.numpy as jnp
from jax import lax
from jax.experimental import pallas as pl
from jax.experimental.pallas import tpu as pltpu
from jax.sharding import PartitionSpec as P

CHUNKS = 2
MESH = pl.DeviceIdType.MESH
NT = (((1,), (1,)), ((), ()))


def kernel(n, width, occ_far, resp_far, cout, proj, occ, r_all, cp, rs, wgt, cs, chome, down, narrow, got,
           last, in_sem, r_send, r_recv, rs_send, rs_recv, ag_send, ag_recv, h_send, h_recv, o_send, o_recv,
           d_send, d_recv, f_send, l_recv):
    bands = occ.shape[0]
    rows, cols = resp_far.shape
    tile = cols // CHUNKS
    me = lax.axis_index("pert")
    mine = lax.axis_index("pw")

    bring_rows = pltpu.make_async_copy(resp_far, r_all.at[me], in_sem.at[0])
    bring_bands = pltpu.make_async_copy(occ_far, occ, in_sem.at[1])
    bring_rows.start()
    bring_bands.start()
    barrier = pltpu.get_barrier_semaphore()
    for k in range(1, n):
        pl.semaphore_signal(barrier, inc=1, device_id={"pert": lax.rem(me + k, n)}, device_id_type=MESH)
    for k in range(1, width):
        pl.semaphore_signal(barrier, inc=1, device_id={"pw": lax.rem(mine + k, width)}, device_id_type=MESH)
    bring_rows.wait()
    pl.semaphore_wait(barrier, n + width - 2)

    def response_copy(q, side):
        return pltpu.make_async_remote_copy(
            src_ref=r_all.at[q], dst_ref=r_all.at[q], send_sem=r_send.at[side, q], recv_sem=r_recv.at[q],
            device_id={"pert": me + 2 * side - 1}, device_id_type=MESH)

    def partial_copy(q, peer):
        return pltpu.make_async_remote_copy(
            src_ref=cp.at[q, peer], dst_ref=rs.at[q, mine], send_sem=rs_send.at[q, peer],
            recv_sem=rs_recv.at[q, mine], device_id={"pw": peer}, device_id_type=MESH)

    def weight_copy(q, peer):
        return pltpu.make_async_remote_copy(
            src_ref=wgt.at[q, mine], dst_ref=wgt.at[q, mine], send_sem=ag_send.at[q, peer],
            recv_sem=ag_recv.at[q, mine], device_id={"pw": peer}, device_id_type=MESH)

    def home_copy(q):
        return pltpu.make_async_remote_copy(
            src_ref=cs.at[q], dst_ref=chome.at[me], send_sem=h_send.at[q], recv_sem=h_recv.at[me],
            device_id={"pert": q}, device_id_type=MESH)

    def spread_copy(j, peer):
        where = cout.at[mine, :, pl.ds(pl.multiple_of(j * bands, 128), bands)]
        return pltpu.make_async_remote_copy(
            src_ref=chome.at[j], dst_ref=where, send_sem=o_send.at[j, peer],
            recv_sem=o_recv.at[j, mine], device_id={"pw": peer}, device_id_type=MESH)

    def narrow_copy(q, c):
        return pltpu.make_async_remote_copy(
            src_ref=narrow.at[q, c], dst_ref=got.at[q, c], send_sem=d_send.at[q, c],
            recv_sem=d_recv.at[q, c], device_id={"pert": jnp.where(q < me, me - 1, me + 1)},
            device_id_type=MESH)

    def last_copy(q, c):
        side = jnp.where(q < me, 0, 1)
        return pltpu.make_async_remote_copy(
            src_ref=narrow.at[q, c], dst_ref=last.at[side, 0, c], send_sem=d_send.at[q, c],
            recv_sem=l_recv.at[side, 0, c], device_id={"pert": q}, device_id_type=MESH)

    def forward_copy(q, c):
        side = jnp.where(q < me, 0, 1)
        return pltpu.make_async_remote_copy(
            src_ref=got.at[q, c], dst_ref=last.at[side, 1, c], send_sem=f_send.at[q, c],
            recv_sem=l_recv.at[side, 1, c], device_id={"pert": q}, device_id_type=MESH)

    def arrived(ref, sem):
        pltpu.make_async_copy(ref, ref, sem).wait()

    def is_next(q):
        return (q == me - 1) | (q == me + 1)

    for side in range(2):
        @pl.when((me > 0) if side == 0 else (me < n - 1))
        def _(side=side):
            response_copy(me, side).start()
    bring_bands.wait()

    def multiply(q):
        part = lax.dot_general(r_all[q], occ[...], NT, preferred_element_type=jnp.float32)
        cp[q] = part.reshape(cp.shape[1:])
        for k in range(1, width):
            partial_copy(q, lax.rem(mine + k, width)).start()
        rs[q, mine] = cp[q, mine]

    def total_up(q):
        for k in range(1, width):
            src = lax.rem(mine + k, width)
            arrived(rs.at[q, src], rs_recv.at[q, src])
        total = rs[q, 0]
        for k in range(1, width):
            total = total + rs[q, k]
        wgt[q, mine] = total.astype(wgt.dtype)
        for k in range(1, width):
            weight_copy(q, lax.rem(mine + k, width)).start()

        @pl.when(q == me)
        def _():
            chome[q] = total

        @pl.when(q != me)
        def _():
            cs[q] = total
            home_copy(q).start()

    def correct(q):
        for k in range(1, width):
            src = lax.rem(mine + k, width)
            arrived(wgt.at[q, src], ag_recv.at[q, src])
        weights = wgt[q].reshape(rows, bands)
        source = ((q < me) & (me == n - 1)) | ((q > me) & (me == 0))
        for c in range(CHUNKS):
            value = jnp.dot(weights, occ[:, c * tile:(c + 1) * tile], preferred_element_type=jnp.float32)

            @pl.when(source | is_next(q))
            def _(c=c, value=value):
                narrow[q, c] = value.astype(narrow.dtype)

            @pl.when(source & is_next(q))
            def _(c=c):
                last_copy(q, c).start()

            @pl.when(source & jnp.logical_not(is_next(q)))
            def _(c=c):
                narrow_copy(q, c).start()

            @pl.when(jnp.logical_not(source | is_next(q)))
            def _(c=c, value=value):
                down[q, c] = value

    def launch(step):
        for side in range(2):
            inner = (me > 0) & (me < n - 1)
            final = n - me if side == 0 else me + 1

            @pl.when(inner & (step == final))
            def _(side=side):
                response_copy(n - 1 if side == 0 else 0, side).wait_send()
                for c in range(CHUNKS):
                    last_copy(me + 2 * side - 1, c).start()

    def relay(step):
        for c in range(CHUNKS):
            for side in range(2):
                q = n - 1 - step if side == 0 else step
                between = ((q < me) & (me < n - 1)) if side == 0 else ((q > me) & (me > 0))

                @pl.when(between)
                def _(c=c, q=q):
                    arrived(got.at[q, c], d_recv.at[q, c])

                    @pl.when(is_next(q))
                    def _():
                        forward_copy(q, c).start()

                    @pl.when(jnp.logical_not(is_next(q)))
                    def _():
                        total = down[q, c] + got[q, c].astype(jnp.float32)
                        narrow[q, c] = total.astype(narrow.dtype)
                        narrow_copy(q, c).start()

    def spread(step):
        def one(side, _):
            j = me + step * (2 * side - 1)

            @pl.when((j >= 0) & (j < n) & ((side == 0) | (step > 0)))
            def _():
                @pl.when(j != me)
                def _():
                    arrived(chome.at[j], h_recv.at[j])

                for k in range(1, width):
                    spread_copy(j, lax.rem(mine + k, width)).start()
                cout[mine, :, pl.ds(pl.multiple_of(j * bands, 128), bands)] = chome[j]
            return 0

        lax.fori_loop(0, 2, one, 0)

    def turn(step, _):
        launch(step)

        def each(stage):
            def one(side, _):
                q = me + step * (2 * side - 1)

                @pl.when((q >= 0) & (q < n) & ((side == 0) | (step > 0)))
                def _():
                    stage(q, side)
                return 0

            lax.fori_loop(0, 2, one, 0)

        def receive(q, side):
            @pl.when(q != me)
            def _():
                arrived(r_all.at[q], r_recv.at[q])

                @pl.when((side == 0) & (me < n - 1))
                def _():
                    response_copy(q, 1).start()

                @pl.when((side == 1) & (me > 0))
                def _():
                    response_copy(q, 0).start()

        each(receive)
        each(lambda q, side: multiply(q))
        each(lambda q, side: total_up(q))
        each(lambda q, side: correct(q))

        @pl.when(step > 0)
        def _():
            relay(step - 1)
            spread(step - 1)
        return 0

    lax.fori_loop(0, n, turn, 0)
    launch(n)
    relay(n - 1)
    spread(n - 1)

    for c in range(CHUNKS):
        at = slice(c * tile, (c + 1) * tile)
        proj[:, at] = down[me, c]

        for side in range(2):
            for k in range(2):
                @pl.when((me < n - 1 - k) if side == 0 else (me > k))
                def _(side=side, k=k, at=at, c=c):
                    arrived(last.at[side, k, c], l_recv.at[side, k, c])
                    proj[:, at] = proj[:, at] + last[side, k, c].astype(jnp.float32)

        proj[:, at] = r_all[me, :, at].astype(jnp.float32) - proj[:, at]

    def drain(q, _):
        for k in range(1, width):
            peer = lax.rem(mine + k, width)
            partial_copy(q, peer).wait_send()
            weight_copy(q, peer).wait_send()
            spread_copy(q, peer).wait_send()
            arrived(cout.at[peer, :, pl.ds(pl.multiple_of(q * bands, 128), bands)], o_recv.at[q, peer])

        inner = (me > 0) & (me < n - 1)

        @pl.when((q >= me) & (me > 0) & jnp.logical_not(inner & (q == n - 1)))
        def _():
            response_copy(q, 0).wait_send()

        @pl.when((q <= me) & (me < n - 1) & jnp.logical_not(inner & (q == 0)))
        def _():
            response_copy(q, 1).wait_send()

        @pl.when(q != me)
        def _():
            home_copy(q).wait_send()
            for c in range(CHUNKS):
                @pl.when(is_next(q))
                def _(c=c):
                    last_copy(q, c).wait_send()

                    @pl.when(inner)
                    def _():
                        forward_copy(q, c).wait_send()

                @pl.when(jnp.logical_not(is_next(q)))
                def _(c=c):
                    narrow_copy(q, c).wait_send()
        return 0

    lax.fori_loop(0, n, drain, 0)


def fused(occupied, rows):
    n, width = lax.axis_size("pert"), lax.axis_size("pw")
    count, cols = rows.shape
    bands = occupied.shape[0]
    part, tile = count // width, cols // CHUNKS
    f32, bf16 = jnp.float32, jnp.bfloat16
    dma = pltpu.SemaphoreType.DMA
    vmem = pl.BlockSpec(memory_space=pltpu.VMEM)
    correlation, projected = pl.pallas_call(
        functools.partial(kernel, n, width),
        out_shape=(
            jax.ShapeDtypeStruct((width, part, n * bands), f32),
            jax.ShapeDtypeStruct((count, cols), f32),
        ),
        in_specs=[pl.BlockSpec(memory_space=pltpu.HBM)] * 2,
        out_specs=(vmem, vmem),
        scratch_shapes=[
            pltpu.VMEM((bands, cols), bf16),
            pltpu.VMEM((n, count, cols), bf16),
            pltpu.VMEM((n, width, part, bands), f32),
            pltpu.VMEM((n, width, part, bands), f32),
            pltpu.VMEM((n, width, part, bands), bf16),
            pltpu.VMEM((n, part, bands), f32),
            pltpu.VMEM((n, part, bands), f32),
            pltpu.VMEM((n, CHUNKS, count, tile), f32),
            pltpu.VMEM((n, CHUNKS, count, tile), bf16),
            pltpu.VMEM((n, CHUNKS, count, tile), bf16),
            pltpu.VMEM((2, 2, CHUNKS, count, tile), bf16),
            dma((2,)), dma((2, n)), dma((n,)),
            dma((n, width)), dma((n, width)),
            dma((n, width)), dma((n, width)),
            dma((n,)), dma((n,)),
            dma((n, width)), dma((n, width)),
            dma((n, CHUNKS)), dma((n, CHUNKS)), dma((n, CHUNKS)), dma((2, 2, CHUNKS)),
        ],
        compiler_params=pltpu.CompilerParams(
            collective_id=0, has_side_effects=True, vmem_limit_bytes=48 * 2**20
        ),
    )(occupied, rows)
    return correlation.reshape(count, n * bands), projected


def ring(occupied, rows):
    band_local = occupied.shape[0]
    n = lax.axis_size("pert")
    position = lax.axis_index("pert")
    zero = jnp.zeros((), jnp.int32)

    def visit(step, piece, correlation, correction):
        start = (position - step) % n * band_local
        part = lax.dot_general(rows, piece, NT, preferred_element_type=jnp.float32)
        summed = lax.psum(part, "pw")
        correlation = lax.dynamic_update_slice(correlation, summed, (zero, start))
        correction = correction + jnp.dot(
            summed.astype(jnp.bfloat16), piece, preferred_element_type=jnp.float32
        )
        return correlation, correction

    def turn(step, state):
        piece, correlation, correction = state
        correlation, correction = visit(step, piece, correlation, correction)
        piece = lax.ppermute(piece, "pert", [(i, (i + 1) % n) for i in range(n)])
        return piece, correlation, correction

    state = (occupied, jnp.zeros((rows.shape[0], n * band_local), jnp.float32), jnp.zeros(rows.shape, jnp.float32))
    piece, correlation, correction = lax.fori_loop(0, n - 1, turn, state)
    correlation, correction = visit(n - 1, piece, correlation, correction)
    return correlation, rows.astype(jnp.float32) - correction


def local(occupied, response):
    rows = response.reshape(-1, response.shape[-1])
    small = rows.shape[0] <= occupied.shape[0]
    even = occupied.shape[0] % 128 == 0 and rows.shape[0] % (16 * lax.axis_size("pw")) == 0
    body = fused if small and even and rows.shape[1] % (128 * CHUNKS) == 0 else ring
    correlation, projected = body(occupied, rows)
    return correlation.reshape(response.shape[:2] + correlation.shape[1:]), projected.reshape(response.shape)


def solution(mesh):
    in_specs = (P(("kpt", "pert"), "pw"), P(("kpt", "pert"), None, "pw"))
    out_specs = (P(("kpt", "pert"), None, None), P(("kpt", "pert"), None, "pw"))
    return jax.shard_map(local, mesh=mesh, in_specs=in_specs, out_specs=out_specs, check_vma=False)
```

```python
import functools

import jax
import jax.numpy as jnp
from jax import lax
from jax.experimental import pallas as pl
from jax.experimental.pallas import tpu as pltpu
from jax.sharding import PartitionSpec as P

CHUNKS = 2
MESH = pl.DeviceIdType.MESH
NT = (((1,), (1,)), ((), ()))


def kernel(n, width, occ_far, resp_far, cout, proj, occ, r_all, cp, rs, wgt, cs, chome, down, narrow, got,
           last, in_sem, r_send, r_recv, rs_send, rs_recv, ag_send, ag_recv, h_send, h_recv, o_send, o_recv,
           d_send, d_recv, f_send, l_recv):
    bands = occ.shape[0]
    rows, cols = resp_far.shape
    tile = cols // CHUNKS
    me = lax.axis_index("pert")
    mine = lax.axis_index("pw")

    bring_rows = pltpu.make_async_copy(resp_far, r_all.at[me], in_sem.at[0])
    bring_bands = pltpu.make_async_copy(occ_far, occ, in_sem.at[1])
    bring_rows.start()
    bring_bands.start()
    barrier = pltpu.get_barrier_semaphore()
    for k in range(1, n):
        pl.semaphore_signal(barrier, inc=1, device_id={"pert": lax.rem(me + k, n)}, device_id_type=MESH)
    for k in range(1, width):
        pl.semaphore_signal(barrier, inc=1, device_id={"pw": lax.rem(mine + k, width)}, device_id_type=MESH)
    bring_rows.wait()
    pl.semaphore_wait(barrier, n + width - 2)

    def response_copy(q, side):
        return pltpu.make_async_remote_copy(
            src_ref=r_all.at[q], dst_ref=r_all.at[q], send_sem=r_send.at[side, q], recv_sem=r_recv.at[q],
            device_id={"pert": me + 2 * side - 1}, device_id_type=MESH)

    def partial_copy(q, peer):
        return pltpu.make_async_remote_copy(
            src_ref=cp.at[q, peer], dst_ref=rs.at[q, mine], send_sem=rs_send.at[q, peer],
            recv_sem=rs_recv.at[q, mine], device_id={"pw": peer}, device_id_type=MESH)

    def weight_copy(q, peer):
        return pltpu.make_async_remote_copy(
            src_ref=wgt.at[q, mine], dst_ref=wgt.at[q, mine], send_sem=ag_send.at[q, peer],
            recv_sem=ag_recv.at[q, mine], device_id={"pw": peer}, device_id_type=MESH)

    def home_copy(q):
        return pltpu.make_async_remote_copy(
            src_ref=cs.at[q], dst_ref=chome.at[me], send_sem=h_send.at[q], recv_sem=h_recv.at[me],
            device_id={"pert": q}, device_id_type=MESH)

    def spread_copy(j, peer):
        where = cout.at[mine, :, pl.ds(pl.multiple_of(j * bands, 128), bands)]
        return pltpu.make_async_remote_copy(
            src_ref=chome.at[j], dst_ref=where, send_sem=o_send.at[j, peer],
            recv_sem=o_recv.at[j, mine], device_id={"pw": peer}, device_id_type=MESH)

    def narrow_copy(q, c):
        return pltpu.make_async_remote_copy(
            src_ref=narrow.at[q, c], dst_ref=got.at[q, c], send_sem=d_send.at[q, c],
            recv_sem=d_recv.at[q, c], device_id={"pert": jnp.where(q < me, me - 1, me + 1)},
            device_id_type=MESH)

    def last_copy(q, c):
        side = jnp.where(q < me, 0, 1)
        return pltpu.make_async_remote_copy(
            src_ref=narrow.at[q, c], dst_ref=last.at[side, 0, c], send_sem=d_send.at[q, c],
            recv_sem=l_recv.at[side, 0, c], device_id={"pert": q}, device_id_type=MESH)

    def forward_copy(q, c):
        side = jnp.where(q < me, 0, 1)
        return pltpu.make_async_remote_copy(
            src_ref=got.at[q, c], dst_ref=last.at[side, 1, c], send_sem=f_send.at[q, c],
            recv_sem=l_recv.at[side, 1, c], device_id={"pert": q}, device_id_type=MESH)

    def arrived(ref, sem):
        pltpu.make_async_copy(ref, ref, sem).wait()

    def is_next(q):
        return (q == me - 1) | (q == me + 1)

    for side in range(2):
        @pl.when((me > 0) if side == 0 else (me < n - 1))
        def _(side=side):
            response_copy(me, side).start()
    bring_bands.wait()

    def multiply(q):
        part = lax.dot_general(r_all[q], occ[...], NT, preferred_element_type=jnp.float32)
        cp[q] = part.reshape(cp.shape[1:])
        for k in range(1, width):
            partial_copy(q, lax.rem(mine + k, width)).start()
        rs[q, mine] = cp[q, mine]

    def total_up(q):
        for k in range(1, width):
            src = lax.rem(mine + k, width)
            arrived(rs.at[q, src], rs_recv.at[q, src])
        total = rs[q, 0]
        for k in range(1, width):
            total = total + rs[q, k]
        wgt[q, mine] = total.astype(wgt.dtype)
        for k in range(1, width):
            weight_copy(q, lax.rem(mine + k, width)).start()

        @pl.when(q == me)
        def _():
            chome[q] = total

        @pl.when(q != me)
        def _():
            cs[q] = total
            home_copy(q).start()

    def correct(q):
        for k in range(1, width):
            src = lax.rem(mine + k, width)
            arrived(wgt.at[q, src], ag_recv.at[q, src])
        weights = wgt[q].reshape(rows, bands)
        source = ((q < me) & (me == n - 1)) | ((q > me) & (me == 0))
        for c in range(CHUNKS):
            value = jnp.dot(weights, occ[:, c * tile:(c + 1) * tile], preferred_element_type=jnp.float32)

            @pl.when(source | is_next(q))
            def _(c=c, value=value):
                narrow[q, c] = value.astype(narrow.dtype)

            @pl.when(source & is_next(q))
            def _(c=c):
                last_copy(q, c).start()

            @pl.when(source & jnp.logical_not(is_next(q)))
            def _(c=c):
                narrow_copy(q, c).start()

            @pl.when(jnp.logical_not(source | is_next(q)))
            def _(c=c, value=value):
                down[q, c] = value

    def launch(step):
        for side in range(2):
            inner = (me > 0) & (me < n - 1)
            final = n - me if side == 0 else me + 1

            @pl.when(inner & (step == final))
            def _(side=side):
                response_copy(n - 1 if side == 0 else 0, side).wait_send()
                for c in range(CHUNKS):
                    last_copy(me + 2 * side - 1, c).start()

    def relay(step):
        for c in range(CHUNKS):
            for side in range(2):
                q = n - 1 - step if side == 0 else step
                between = ((q < me) & (me < n - 1)) if side == 0 else ((q > me) & (me > 0))

                @pl.when(between)
                def _(c=c, q=q):
                    arrived(got.at[q, c], d_recv.at[q, c])

                    @pl.when(is_next(q))
                    def _():
                        forward_copy(q, c).start()

                    @pl.when(jnp.logical_not(is_next(q)))
                    def _():
                        total = down[q, c] + got[q, c].astype(jnp.float32)
                        narrow[q, c] = total.astype(narrow.dtype)
                        narrow_copy(q, c).start()

    def spread(step):
        def one(side, _):
            j = me + step * (2 * side - 1)

            @pl.when((j >= 0) & (j < n) & ((side == 0) | (step > 0)))
            def _():
                @pl.when(j != me)
                def _():
                    arrived(chome.at[j], h_recv.at[j])

                for k in range(1, width):
                    spread_copy(j, lax.rem(mine + k, width)).start()
                cout[mine, :, pl.ds(pl.multiple_of(j * bands, 128), bands)] = chome[j]
            return 0

        lax.fori_loop(0, 2, one, 0)

    def turn(step, _):
        launch(step)

        def each(stage):
            def one(side, _):
                q = me + step * (2 * side - 1)

                @pl.when((q >= 0) & (q < n) & ((side == 0) | (step > 0)))
                def _():
                    stage(q, side)
                return 0

            lax.fori_loop(0, 2, one, 0)

        def receive(q, side):
            @pl.when(q != me)
            def _():
                arrived(r_all.at[q], r_recv.at[q])

                @pl.when((side == 0) & (me < n - 1))
                def _():
                    response_copy(q, 1).start()

                @pl.when((side == 1) & (me > 0))
                def _():
                    response_copy(q, 0).start()

        each(receive)
        each(lambda q, side: multiply(q))
        each(lambda q, side: total_up(q))
        each(lambda q, side: correct(q))

        @pl.when(step > 0)
        def _():
            relay(step - 1)
            spread(step - 1)
        return 0

    lax.fori_loop(0, n, turn, 0)
    launch(n)
    relay(n - 1)
    spread(n - 1)

    for c in range(CHUNKS):
        at = slice(c * tile, (c + 1) * tile)
        proj[:, at] = down[me, c]

        for side in range(2):
            for k in range(2):
                @pl.when((me < n - 1 - k) if side == 0 else (me > k))
                def _(side=side, k=k, at=at, c=c):
                    arrived(last.at[side, k, c], l_recv.at[side, k, c])
                    proj[:, at] = proj[:, at] + last[side, k, c].astype(jnp.float32)

        proj[:, at] = r_all[me, :, at].astype(jnp.float32) - proj[:, at]

    def drain(q, _):
        for k in range(1, width):
            peer = lax.rem(mine + k, width)
            partial_copy(q, peer).wait_send()
            weight_copy(q, peer).wait_send()
            spread_copy(q, peer).wait_send()
            arrived(cout.at[peer, :, pl.ds(pl.multiple_of(q * bands, 128), bands)], o_recv.at[q, peer])

        inner = (me > 0) & (me < n - 1)

        @pl.when((q >= me) & (me > 0) & jnp.logical_not(inner & (q == n - 1)))
        def _():
            response_copy(q, 0).wait_send()

        @pl.when((q <= me) & (me < n - 1) & jnp.logical_not(inner & (q == 0)))
        def _():
            response_copy(q, 1).wait_send()

        @pl.when(q != me)
        def _():
            home_copy(q).wait_send()
            for c in range(CHUNKS):
                @pl.when(is_next(q))
                def _(c=c):
                    last_copy(q, c).wait_send()

                    @pl.when(inner)
                    def _():
                        forward_copy(q, c).wait_send()

                @pl.when(jnp.logical_not(is_next(q)))
                def _(c=c):
                    narrow_copy(q, c).wait_send()
        return 0

    lax.fori_loop(0, n, drain, 0)


def fused(occupied, rows):
    n, width = lax.axis_size("pert"), lax.axis_size("pw")
    count, cols = rows.shape
    bands = occupied.shape[0]
    part, tile = count // width, cols // CHUNKS
    f32, bf16 = jnp.float32, jnp.bfloat16
    dma = pltpu.SemaphoreType.DMA
    vmem = pl.BlockSpec(memory_space=pltpu.VMEM)
    correlation, projected = pl.pallas_call(
        functools.partial(kernel, n, width),
        out_shape=(
            jax.ShapeDtypeStruct((width, part, n * bands), f32),
            jax.ShapeDtypeStruct((count, cols), f32),
        ),
        in_specs=[pl.BlockSpec(memory_space=pltpu.HBM)] * 2,
        out_specs=(vmem, vmem),
        scratch_shapes=[
            pltpu.VMEM((bands, cols), bf16),
            pltpu.VMEM((n, count, cols), bf16),
            pltpu.VMEM((n, width, part, bands), f32),
            pltpu.VMEM((n, width, part, bands), f32),
            pltpu.VMEM((n, width, part, bands), bf16),
            pltpu.VMEM((n, part, bands), f32),
            pltpu.VMEM((n, part, bands), f32),
            pltpu.VMEM((n, CHUNKS, count, tile), f32),
            pltpu.VMEM((n, CHUNKS, count, tile), bf16),
            pltpu.VMEM((n, CHUNKS, count, tile), bf16),
            pltpu.VMEM((2, 2, CHUNKS, count, tile), bf16),
            dma((2,)), dma((2, n)), dma((n,)),
            dma((n, width)), dma((n, width)),
            dma((n, width)), dma((n, width)),
            dma((n,)), dma((n,)),
            dma((n, width)), dma((n, width)),
            dma((n, CHUNKS)), dma((n, CHUNKS)), dma((n, CHUNKS)), dma((2, 2, CHUNKS)),
        ],
        compiler_params=pltpu.CompilerParams(
            collective_id=0, has_side_effects=True, vmem_limit_bytes=51 * 2**20
        ),
    )(occupied, rows)
    return correlation.reshape(count, n * bands), projected


def ring(occupied, rows):
    band_local = occupied.shape[0]
    n = lax.axis_size("pert")
    position = lax.axis_index("pert")
    zero = jnp.zeros((), jnp.int32)

    def visit(step, piece, correlation, correction):
        start = (position - step) % n * band_local
        part = lax.dot_general(rows, piece, NT, preferred_element_type=jnp.float32)
        summed = lax.psum(part, "pw")
        correlation = lax.dynamic_update_slice(correlation, summed, (zero, start))
        correction = correction + jnp.dot(
            summed.astype(jnp.bfloat16), piece, preferred_element_type=jnp.float32
        )
        return correlation, correction

    def turn(step, state):
        piece, correlation, correction = state
        correlation, correction = visit(step, piece, correlation, correction)
        piece = lax.ppermute(piece, "pert", [(i, (i + 1) % n) for i in range(n)])
        return piece, correlation, correction

    state = (occupied, jnp.zeros((rows.shape[0], n * band_local), jnp.float32), jnp.zeros(rows.shape, jnp.float32))
    piece, correlation, correction = lax.fori_loop(0, n - 1, turn, state)
    correlation, correction = visit(n - 1, piece, correlation, correction)
    return correlation, rows.astype(jnp.float32) - correction


def local(occupied, response):
    rows = response.reshape(-1, response.shape[-1])
    small = rows.shape[0] <= occupied.shape[0]
    even = occupied.shape[0] % 128 == 0 and rows.shape[0] % (16 * lax.axis_size("pw")) == 0
    body = fused if small and even and rows.shape[1] % (128 * CHUNKS) == 0 else ring
    correlation, projected = body(occupied, rows)
    return correlation.reshape(response.shape[:2] + correlation.shape[1:]), projected.reshape(response.shape)


def solution(mesh):
    in_specs = (P(("kpt", "pert"), "pw"), P(("kpt", "pert"), None, "pw"))
    out_specs = (P(("kpt", "pert"), None, None), P(("kpt", "pert"), None, "pw"))
    return jax.shard_map(local, mesh=mesh, in_specs=in_specs, out_specs=out_specs, check_vma=False)
```
